32 devices in a mesh: row: 4 (over y, x), col: 8 (over z, core).
Axes of the slice: x: 2, y: 2, z: 4, core: 2. Of those that a mesh axis runs over, the one named last changes fastest.
Arguments:
- out_grad: bfloat16 [512, 6144], P('row', 'col'), may hold values from -6 to 6
- hidden: bfloat16 [512, 24576], P('row'), may hold values from -0.1796875 to 0.1796875
- weight: bfloat16 [24576, 6144], P('row', 'col'), may hold values from -0.078125 to 0.078125
- compress: bfloat16 [512, 128], replicated, may hold values from -0.25 to 0.25
- feedback: bfloat16 [8, 512, 24576], P('col', None, 'row'), may hold values from -1.5 to 1.5
Outputs:
- grad_input: bfloat16 [512, 24576], P('col', 'row')
- grad_weight: bfloat16 [24576, 6144], P('row', 'col')
- new_feedback: bfloat16 [8, 512, 24576], P('col', None, 'row')
The draws below stay inside these ranges and needn't reach their ends.
All inputs are finite; a program needn't handle non-finite values.
Results may differ from the reference program's by a relative error of at most 0.0056.
Values may be sent and summed in bfloat16 or wider, within the bound.
No kernel may reach another device: no remote copies, remote signals or barrier semaphores. Data moves between devices by JAX's collectives and lax.ppermute only.
A program may use at most 256 MiB of HBM per device.

```python
import jax
import jax.numpy as jnp
from jax import lax

D = 6144
FF = 24576
BLK = 512
SUB = 128
TOKENS = 512
N_COL = 8


def strengthened(array, key, source, target, blocks, factor):
    def block_of(axis_at):
        return (jnp.arange(array.shape[axis_at]) // (array.shape[axis_at] // blocks)).reshape((-1,) + (1,) * (array.ndim - 1 - axis_at))

    near = jax.random.permutation(key, blocks)[block_of(target)]
    other_side = (block_of(target) + blocks // 2) % blocks
    return jnp.where((block_of(source) == near) | (block_of(source) == other_side), factor * array, array)


def block_levels(key, dims, cuts, least, top_value):
    def one(dim, shards_of):
        steps = jax.random.uniform(jax.random.fold_in(jax.random.fold_in(key, 6), dim), (shards_of,), jnp.float32, least / len(cuts), top_value / len(cuts))
        return jnp.repeat(jnp.exp(steps), dims[dim] // shards_of).reshape((-1,) + (1,) * (len(dims) - dim - 1))

    loudness = one(*cuts[0])
    for cut in cuts[1:]:
        loudness = loudness * one(*cut)
    return loudness


def bell_draw(stream_key, dims, scale, most, split=(), held_as=jnp.bfloat16):
    array = jax.random.normal(stream_key, dims, jnp.float32) * scale
    if len(split) > 0:
        array = block_levels(stream_key, dims, split, -0.22, 0.18) * array
    return jnp.clip(array, min=-most, max=most).astype(held_as)


def heavy_noise(stream_key, dims, deviation, bound, pieces, heavy, held_as=jnp.bfloat16):
    array = deviation * jax.random.normal(stream_key, dims, jnp.float32)
    if pieces:
        array = array * block_levels(stream_key, dims, pieces, -0.22, 0.18)
    return jnp.clip(strengthened(array, jax.random.fold_in(stream_key, 3), *heavy), -bound, bound).astype(held_as)


def setup_inputs(seed: int = 0) -> dict:
    arg_keys = jax.random.split(jax.random.key(seed), 6)
    return {
        "out_grad": bell_draw(arg_keys[0], (TOKENS, D), 1.0, 6.0, ((0, 4), (1, 8))),
        "hidden": heavy_noise(arg_keys[1], (TOKENS, FF), 0.03, 0.1796875, ((0, 4),), (0, 1, 4, 2.0)),
        "weight": bell_draw(arg_keys[2], (FF, D), D ** -0.5, 0.078125, ((0, 4), (1, 8))),
        "compress": bell_draw(arg_keys[3], (BLK, SUB), BLK ** -0.5, 0.25),
        "feedback": bell_draw(arg_keys[4], (N_COL, TOKENS, FF), 0.25, 1.5, ((0, 8), (2, 4))),
    }


def reference(out_grad, hidden, weight, compress, feedback):
    width = D // N_COL
    weight_cols = weight.reshape(FF, N_COL, width).transpose(1, 0, 2)
    grad_cols = out_grad.reshape(TOKENS, N_COL, width).transpose(1, 0, 2)
    comp = compress.astype(jnp.float32)

    def one_col(total, inputs):
        grads, wcols, resid = inputs
        partial_value = lax.dot_general(grads, wcols, (((1,), (1,)), ((), ())), preferred_element_type=jnp.float32)
        acc = partial_value + resid.astype(jnp.float32)
        blocks = acc.astype(jnp.bfloat16).astype(jnp.float32).reshape(TOKENS, FF // BLK, BLK)
        code = jnp.einsum('tnb,bs->tns', blocks, comp)
        code_low = code.astype(jnp.bfloat16).astype(jnp.float32)
        recon = jnp.einsum('tns,bs->tnb', code_low, comp).reshape(TOKENS, FF)
        fresh = (acc - recon).astype(jnp.bfloat16)
        return total + code, fresh

    start = jnp.zeros((TOKENS, FF // BLK, SUB), jnp.float32)
    total, new_feedback = lax.scan(one_col, start, (grad_cols, weight_cols, feedback))
    total_low = total.astype(jnp.bfloat16).astype(jnp.float32)
    grad_input = jnp.einsum('tns,bs->tnb', total_low, comp).reshape(TOKENS, FF).astype(jnp.bfloat16)
    grad_weight = jnp.dot(hidden.T, out_grad, preferred_element_type=jnp.float32).astype(jnp.bfloat16)
    return grad_input, grad_weight, new_feedback
```

```python
import functools

import jax
import jax.numpy as jnp
from jax import lax
from jax.experimental import pallas as pl
from jax.experimental.pallas import tpu as pltpu
from jax.sharding import PartitionSpec as P

F32 = jnp.float32
BF16 = jnp.bfloat16
MIB = 1024 * 1024
GW_BLOCKS = 4
LONG = pl.CostEstimate(flops=1 << 36, bytes_accessed=1 << 28, transcendentals=0)
COST = pl.CostEstimate(flops=1, bytes_accessed=1, transcendentals=0)


def in_hbm(*arrays):
    return [pltpu.with_memory_space_constraint(x, pltpu.HBM) for x in arrays]


def xor_perm(n, k):
    return [(i, i ^ k) for i in range(n)]


def place(i, count):
    bits = count.bit_length() - 1
    return sum(((i >> b) & 1) << (bits - 1 - b) for b in range(bits))


def compress_kernel(nrow, ncol, idx_ref, *refs):
    pieces = refs[:nrow]
    weight_ref, feedback_ref, compress_ref = refs[nrow : nrow + 3]
    fresh_ref, *code_refs, ordered_ref, grads, acc_buf, code_buf, sems = refs[nrow + 3 :]
    row, core = idx_ref[0], idx_ref[1]
    step_tokens = pieces[0].shape[0]
    blk, sub = compress_ref.shape
    count = weight_ref.shape[0] // blk

    def rows_at(i):
        return pl.ds(pl.multiple_of(i * step_tokens, step_tokens), step_tokens)

    def slot(k):
        if k == 0:
            return 0
        if k == nrow - 1:
            return 1
        return k + 1 + core if k % 2 else k - core + 1

    passed = [
        pltpu.make_async_copy(pieces[k], ordered_ref.at[rows_at(slot(k)), :], sems.at[k])
        for k in range(nrow)
    ]

    @pl.when(pl.program_id(0) == 0)
    def _():
        for copy in passed:
            copy.start()
        for k in range(nrow):
            grads[rows_at(row ^ k), :] = pieces[k][...]

    def product(b):
        cols = slice(b * blk, (b + 1) * blk)
        partial = lax.dot_general(
            grads[...], weight_ref[cols, :], (((1,), (1,)), ((), ())), preferred_element_type=F32
        )
        acc_buf[b] = partial + feedback_ref[0, :, cols].astype(F32)

    def finish(b):
        acc = acc_buf[b]
        code = jnp.dot(acc.astype(BF16), compress_ref[...], preferred_element_type=F32)
        code_low = code.astype(BF16)
        code_buf[:, b * sub : (b + 1) * sub] = code_low
        recon = lax.dot_general(
            code_low, compress_ref[...], (((1,), (1,)), ((), ())), preferred_element_type=F32
        )
        fresh_ref[0, :, b * blk : (b + 1) * blk] = (acc - recon).astype(BF16)

    for b in range(count):
        product(b)
        if b:
            finish(b - 1)
    finish(count - 1)

    mine_tokens = grads.shape[0] // ncol
    width = count * sub
    cols = pl.ds(pl.multiple_of(pl.program_id(0) * width, width), width)
    for i in range(ncol // 2):
        which, to = divmod(place(i, ncol // 2), ncol // 4)
        z = idx_ref[2] ^ i
        for whose, refs_of in ((core, code_refs[:2]), (1 - core, code_refs[2:])):
            at = pl.multiple_of((2 * z + whose) * mine_tokens, mine_tokens)
            refs_of[which][to * mine_tokens : (to + 1) * mine_tokens, cols] = code_buf[
                pl.ds(at, mine_tokens), :
            ]

    @pl.when(pl.program_id(0) == pl.num_programs(0) - 1)
    def _():
        for copy in passed:
            copy.wait()


def compress_call(idx, pieces, weight, feedback, compress, ncol):
    nrow = len(pieces)
    units, width = weight.shape
    blk, sub = compress.shape
    tokens = feedback.shape[1]
    nblocks = units // blk
    quarter = tokens // 4
    per = 3 if nblocks % 3 == 0 else 1
    return pl.pallas_call(
        functools.partial(compress_kernel, nrow, ncol),
        grid_spec=pltpu.PrefetchScalarGridSpec(
            num_scalar_prefetch=1,
            grid=(nblocks // per,),
            in_specs=[pl.BlockSpec((tokens // nrow, width), lambda j, s: (0, 0))]
            + [pl.BlockSpec(memory_space=pltpu.VMEM)] * (nrow - 1)
            + [
                pl.BlockSpec((per * blk, width), lambda j, s: (j, 0)),
                pl.BlockSpec((1, tokens, per * blk), lambda j, s: (0, 0, j)),
                pl.BlockSpec((blk, sub), lambda j, s: (0, 0)),
            ],
            out_specs=[pl.BlockSpec((1, tokens, per * blk), lambda j, s: (0, 0, j))]
            + [pl.BlockSpec(memory_space=pltpu.VMEM)] * 4
            + [pl.BlockSpec(memory_space=pl.ANY)],
            scratch_shapes=[
                pltpu.VMEM((tokens, width), BF16),
                pltpu.VMEM((per, tokens, blk), F32),
                pltpu.VMEM((tokens, per * sub), BF16),
                pltpu.SemaphoreType.DMA((nrow,)),
            ],
        ),
        out_shape=[pltpu.HBM((1, tokens, units), BF16)]
        + [jax.ShapeDtypeStruct((quarter, nblocks * sub), BF16)] * 4
        + [pltpu.HBM((tokens, width), BF16)],
        compiler_params=pltpu.CompilerParams(vmem_limit_bytes=30 * MIB),
        cost_estimate=LONG,
        name="compress_codes",
    )(idx, *in_hbm(pieces[0]), *pieces[1:], *in_hbm(weight, feedback, compress))


def pack_kernel(parts, idx_ref, hidden_ref, *refs):
    outs, (buf, sems) = refs[:-2], refs[-2:]
    arriving, leaving = [], []
    at = 0
    for i, (out, first, low, length) in enumerate(parts):
        source = pl.ds(pl.multiple_of(first(idx_ref[0], idx_ref[1]) + low, 128), length)
        held = buf.at[:, at : at + length]
        arriving.append(pltpu.make_async_copy(hidden_ref.at[:, source], held, sems.at[0, i]))
        leaving.append(
            pltpu.make_async_copy(held, outs[out].at[:, low : low + length], sems.at[1, i])
        )
        at += length
    for copy in arriving:
        copy.start()
    for copy, then in zip(arriving, leaving):
        copy.wait()
        then.start()
    for copy in leaving:
        copy.wait()


def pack_call(idx, hidden, firsts, lengths):
    step = min(lengths)
    parts = [
        (i, first, low, step)
        for i, (first, length) in enumerate(zip(firsts, lengths))
        for low in range(0, length, step)
    ]
    step_tokens = hidden.shape[0]
    return pl.pallas_call(
        functools.partial(pack_kernel, parts),
        grid_spec=pltpu.PrefetchScalarGridSpec(
            num_scalar_prefetch=1,
            grid=(1,),
            in_specs=[pl.BlockSpec(memory_space=pl.ANY)],
            out_specs=[pl.BlockSpec(memory_space=pl.ANY)] * len(firsts),
            scratch_shapes=[
                pltpu.VMEM((step_tokens, sum(lengths)), BF16),
                pltpu.SemaphoreType.DMA((2, len(parts))),
            ],
        ),
        out_shape=[pltpu.HBM((step_tokens, n), BF16) for n in lengths],
        compiler_params=pltpu.CompilerParams(vmem_limit_bytes=10 * MIB),
        cost_estimate=COST,
        name="pack_hidden",
    )(idx, *in_hbm(hidden))


def gw_kernel(npieces, steps, idx_ref, own_ref, diag_ref, swapped_ref, *refs):
    pieces = refs[:npieces]
    grads_ref = refs[npieces]
    out_ref, lhs = refs[-2:]
    step_tokens, block = own_ref.shape
    j = pl.program_id(0)
    core = idx_ref[1]

    def put(slot, x):
        lhs[slot * step_tokens : (slot + 1) * step_tokens, :] = x

    def columns(i):
        return pl.ds(pl.multiple_of(i * block, block), block)

    put(0, own_ref[...])
    for i, piece in enumerate(pieces):
        put(2 + i, piece[:, columns(gw_block(j, core, steps))])

    @pl.when(j < steps)
    def _():
        put(1, diag_ref[:, columns(j)])

    @pl.when(j >= steps)
    def _():
        put(1, swapped_ref[:, columns(j - steps)])

    out_ref[...] = lax.dot_general(
        lhs[...], grads_ref[...], (((0,), (0,)), ((), ())), preferred_element_type=F32
    ).astype(BF16)


def gw_block(j, core, steps):
    return jnp.where(j < steps, core, 1 - core) * steps + lax.rem(j, steps)


def gw_call(idx, hidden, diag, swapped, pieces, grads, prev, low, units):
    tokens, width = grads.shape
    step_tokens, half = diag.shape
    block = units // GW_BLOCKS
    steps = half // block
    at_low = low // block

    def at(j, s):
        return at_low + gw_block(j, s[1], steps)

    in_specs = [pl.BlockSpec((step_tokens, block), lambda j, s: (0, s[0] * GW_BLOCKS + at(j, s)))]
    in_specs += [pl.BlockSpec(memory_space=pltpu.VMEM)] * (2 + len(pieces))
    in_specs += [pl.BlockSpec((tokens, width), lambda j, s: (0, 0))]
    args = [*in_hbm(hidden), diag, swapped, *pieces, *in_hbm(grads)]
    aliases = {}
    if prev is not None:
        in_specs += [pl.BlockSpec(memory_space=pl.ANY)]
        args += [prev]
        aliases = {len(args): 0}
    return pl.pallas_call(
        functools.partial(gw_kernel, len(pieces), steps),
        grid_spec=pltpu.PrefetchScalarGridSpec(
            num_scalar_prefetch=1,
            grid=(2 * steps,),
            in_specs=in_specs,
            out_specs=pl.BlockSpec((block, width), lambda j, s: (at(j, s), 0)),
            scratch_shapes=[pltpu.VMEM((tokens, block), BF16)],
        ),
        out_shape=pltpu.HBM((units, width), BF16),
        input_output_aliases=aliases,
        compiler_params=pltpu.CompilerParams(vmem_limit_bytes=28 * MIB),
        cost_estimate=COST,
        name="weight_gradient",
    )(idx, *args)


def gi_kernel(own_ref, *refs):
    recv = refs[:-2]
    compress_ref, out_ref = refs[-2:]
    total = own_ref[...]
    for piece in recv:
        total = total + piece[...].astype(F32)
    low = total.astype(BF16)
    blk, sub = compress_ref.shape
    for n in range(low.shape[1] // sub):
        out_ref[:, n * blk : (n + 1) * blk] = lax.dot_general(
            low[:, n * sub : (n + 1) * sub],
            compress_ref[...],
            (((1,), (1,)), ((), ())),
            preferred_element_type=F32,
        ).astype(BF16)


def gi_call(own, recv, compress, units):
    tokens, codes = own.shape
    blk, sub = compress.shape
    nblocks = codes // sub
    per = nblocks // 3 if nblocks % 3 == 0 else 1
    spec = pl.BlockSpec((tokens, per * sub), lambda j: (0, j))
    return pl.pallas_call(
        gi_kernel,
        grid=(nblocks // per,),
        in_specs=[spec] * (1 + len(recv)) + [pl.BlockSpec((blk, sub), lambda j: (0, 0))],
        out_specs=pl.BlockSpec((tokens, per * blk), lambda j: (0, j)),
        out_shape=pltpu.HBM((tokens, units), BF16),
        compiler_params=pltpu.CompilerParams(vmem_limit_bytes=10 * MIB),
        cost_estimate=LONG,
        name="grad_input",
    )(own, *recv, compress)


def on_device(nrow, ncol, out_grad, hidden, weight, compress, feedback):
    row = lax.axis_index("row")
    col = lax.axis_index("col")
    core = col % 2
    units = weight.shape[0]
    step_tokens = out_grad.shape[0]
    after = lax.optimization_barrier

    def over_row(x, k):
        return lax.ppermute(x, "row", xor_perm(nrow, k))

    def over_col(x, k):
        return lax.ppermute(x, "col", xor_perm(ncol, k))

    idx = jnp.stack([row, core, col // 2]).astype(jnp.int32)
    grads = [out_grad] + [over_row(out_grad, k) for k in range(1, nrow)]

    def joint_perm(k):
        return [
            (r * ncol + c, (r ^ (k + c % 2)) * ncol + c) for r in range(nrow) for c in range(ncol)
        ]

    pairs = range(1, nrow - 1, 2)
    lows, lengths = [0, units // 2], [units // 2] * 2
    firsts, sizes = [], []
    for low, length in zip(lows, lengths):
        firsts += [lambda r, e, k=k, low=low: (r ^ (k + e)) * units + low for k in pairs]
        firsts += [
            lambda r, e, low=low, half=length // 2: (r ^ (nrow - 1)) * units + low + e * half
        ]
        sizes += [length] * len(pairs) + [length // 2]
    packed = pack_call(idx, hidden, firsts, sizes)

    def fetch(parts):
        fetched = [lax.ppermute(x, ("row", "col"), joint_perm(k)) for k, x in zip(pairs, parts)]
        return fetched + [over_row(parts[-1], nrow - 1)]

    def swap(parts):
        swapped = [over_col(x, 1) for x in parts]
        return parts[-1], swapped[-1], [x for pair in zip(parts[:-1], swapped[:-1]) for x in pair]

    early = fetch(packed[: len(pairs) + 1])
    new_feedback, *codes, ordered = compress_call(idx, grads, weight, feedback, compress, ncol)
    late = fetch(packed[len(pairs) + 1 :])

    *others, kept, send = after((*early, *[over_col(x, 1) for x in codes[2:]]))
    early = swap(others)
    kept, send = [x.astype(F32) + y.astype(F32) for x, y in zip(codes[:2], (kept, send))]
    step = 1
    while True:
        received = over_col(send.astype(BF16), 2 * step)
        step *= 2
        if step == ncol // 2:
            break
        size = kept.shape[0] // 2
        send = kept[size:] + received[size:].astype(F32)
        kept = kept[:size] + received[:size].astype(F32)

    grad_weight = gw_call(idx, hidden, *early, ordered, None, lows[0], units)
    grad_weight, kept, *late = after((grad_weight, kept, *late))
    grad_input = gi_call(kept, [received], compress, units)
    diag, swapped, pieces = swap(late)
    grad_input, swapped, *pieces = after((grad_input, swapped, *pieces))
    grad_weight = gw_call(idx, hidden, diag, swapped, pieces, ordered, grad_weight, lows[1], units)
    return (grad_input, grad_weight, new_feedback)


def solution(mesh):
    return jax.shard_map(
        functools.partial(on_device, mesh.shape["row"], mesh.shape["col"]),
        mesh=mesh,
        in_specs=(P("row", "col"), P("row", None), P("row", "col"), P(), P("col", None, "row")),
        out_specs=(P("col", "row"), P("row", "col"), P("col", None, "row")),
        check_vma=False,
    )
```

```python
import functools

import jax
import jax.numpy as jnp
from jax import lax
from jax.experimental import pallas as pl
from jax.experimental.pallas import tpu as pltpu
from jax.sharding import PartitionSpec as P

F32 = jnp.float32
BF16 = jnp.bfloat16
MIB = 1024 * 1024
GW_BLOCKS = 8
LONG = pl.CostEstimate(flops=1 << 36, bytes_accessed=1 << 28, transcendentals=0)
COST = pl.CostEstimate(flops=1, bytes_accessed=1, transcendentals=0)


def in_hbm(*arrays):
    return [pltpu.with_memory_space_constraint(x, pltpu.HBM) for x in arrays]


def xor_perm(n, k):
    return [(i, i ^ k) for i in range(n)]


def place(i, count):
    bits = count.bit_length() - 1
    return sum(((i >> b) & 1) << (bits - 1 - b) for b in range(bits))


def compress_kernel(nrow, ncol, group, idx_ref, *refs):
    pieces = [refs[0], *refs[1:nrow]]
    weight_hbm, feedback_hbm, compress_ref, fresh_hbm = refs[nrow : nrow + 4]
    *code_refs, ordered_ref = refs[nrow + 4 : nrow + 9]
    weight, feedback, fresh, grads, acc_buf, code_buf, in_sems, out_sems, sems = refs[nrow + 9 :]
    row, core = idx_ref[0], idx_ref[1]
    step_tokens = pieces[0].shape[0]
    blk, sub = compress_ref.shape
    nblocks = weight.shape[0]
    mine_tokens = grads.shape[0] // ncol

    def rows_at(i):
        return pl.ds(pl.multiple_of(i * step_tokens, step_tokens), step_tokens)

    def slot(k):
        if k == 0:
            return 0
        if k == nrow - 1:
            return 1
        return k + 1 + core if k % 2 else k - core + 1

    def span(n):
        return pl.ds(pl.multiple_of(n * blk, blk), blk)

    def arriving(n):
        return (
            pltpu.make_async_copy(weight_hbm.at[span(n), :], weight.at[n], in_sems.at[0, n]),
            pltpu.make_async_copy(feedback_hbm.at[0, :, span(n)], feedback.at[n], in_sems.at[1, n]),
        )

    def leaving(n):
        return pltpu.make_async_copy(fresh.at[n], fresh_hbm.at[0, :, span(n)], out_sems.at[n])

    @pl.loop(0, nblocks)
    def _(n):
        for copy in arriving(n):
            copy.start()

    passed = [
        pltpu.make_async_copy(pieces[k], ordered_ref.at[rows_at(slot(k)), :], sems.at[k])
        for k in range(nrow)
    ]
    for copy in passed:
        copy.start()
    for k in range(nrow):
        grads[rows_at(row ^ k), :] = pieces[k][...]

    def product(n, b):
        for copy in arriving(n):
            copy.wait()
        partial = lax.dot_general(
            grads[...], weight[n], (((1,), (1,)), ((), ())), preferred_element_type=F32
        )
        acc_buf[b] = partial + feedback[n].astype(F32)

    def finish(n, b):
        acc = acc_buf[b]
        code = jnp.dot(acc.astype(BF16), compress_ref[...], preferred_element_type=F32)
        code_low = code.astype(BF16)
        code_buf[:, b * sub : (b + 1) * sub] = code_low
        recon = lax.dot_general(
            code_low, compress_ref[...], (((1,), (1,)), ((), ())), preferred_element_type=F32
        )
        fresh[n] = (acc - recon).astype(BF16)
        leaving(n).start()

    @pl.loop(0, nblocks // group)
    def _(g):
        for b in range(group):
            product(g * group + b, b)
            if b:
                finish(g * group + b - 1, b - 1)
        finish(g * group + group - 1, group - 1)
        width = group * sub
        cols = pl.ds(pl.multiple_of(g * width, width), width)
        for i in range(ncol // 2):
            which, to = divmod(place(i, ncol // 2), ncol // 4)
            z = idx_ref[2] ^ i
            for whose, refs_of in ((core, code_refs[:2]), (1 - core, code_refs[2:])):
                at = pl.multiple_of((2 * z + whose) * mine_tokens, mine_tokens)
                refs_of[which][to * mine_tokens : (to + 1) * mine_tokens, cols] = code_buf[
                    pl.ds(at, mine_tokens), :
                ]

    for copy in passed:
        copy.wait()

    @pl.loop(0, nblocks)
    def _(n):
        leaving(n).wait()


def compress_call(idx, pieces, weight, feedback, compress, ncol):
    nrow = len(pieces)
    units, width = weight.shape
    blk, sub = compress.shape
    tokens = feedback.shape[1]
    nblocks = units // blk
    quarter = tokens // 4
    group = 3 if nblocks % 3 == 0 else 1
    return pl.pallas_call(
        functools.partial(compress_kernel, nrow, ncol, group),
        grid_spec=pltpu.PrefetchScalarGridSpec(
            num_scalar_prefetch=1,
            grid=(1,),
            in_specs=[pl.BlockSpec((tokens // nrow, width), lambda j, s: (0, 0))]
            + [pl.BlockSpec(memory_space=pltpu.VMEM)] * (nrow - 1)
            + [pl.BlockSpec(memory_space=pl.ANY)] * 2
            + [pl.BlockSpec((blk, sub), lambda j, s: (0, 0))],
            out_specs=[pl.BlockSpec(memory_space=pl.ANY)]
            + [pl.BlockSpec(memory_space=pltpu.VMEM)] * 4
            + [pl.BlockSpec(memory_space=pl.ANY)],
            scratch_shapes=[
                pltpu.VMEM((nblocks, blk, width), BF16),
                pltpu.VMEM((nblocks, tokens, blk), BF16),
                pltpu.VMEM((nblocks, tokens, blk), BF16),
                pltpu.VMEM((tokens, width), BF16),
                pltpu.VMEM((group, tokens, blk), F32),
                pltpu.VMEM((tokens, group * sub), BF16),
                pltpu.SemaphoreType.DMA((2, nblocks)),
                pltpu.SemaphoreType.DMA((nblocks,)),
                pltpu.SemaphoreType.DMA((nrow,)),
            ],
        ),
        out_shape=[pltpu.HBM((1, tokens, units), BF16)]
        + [jax.ShapeDtypeStruct((quarter, nblocks * sub), BF16)] * 4
        + [pltpu.HBM((tokens, width), BF16)],
        compiler_params=pltpu.CompilerParams(vmem_limit_bytes=44 * MIB),
        cost_estimate=LONG,
        name="compress_codes",
    )(idx, *in_hbm(pieces[0]), *pieces[1:], *in_hbm(weight, feedback, compress))


def pack_kernel(parts, idx_ref, hidden_ref, *refs):
    outs, (buf, sems) = refs[:-2], refs[-2:]
    arriving, leaving = [], []
    at = 0
    for i, (out, first, low, length) in enumerate(parts):
        source = pl.ds(pl.multiple_of(first(idx_ref[0], idx_ref[1]) + low, 128), length)
        held = buf.at[:, at : at + length]
        arriving.append(pltpu.make_async_copy(hidden_ref.at[:, source], held, sems.at[0, i]))
        leaving.append(
            pltpu.make_async_copy(held, outs[out].at[:, low : low + length], sems.at[1, i])
        )
        at += length
    for copy in arriving:
        copy.start()
    for copy, then in zip(arriving, leaving):
        copy.wait()
        then.start()
    for copy in leaving:
        copy.wait()


def pack_call(idx, hidden, firsts, lengths):
    step = min(lengths)
    parts = [
        (i, first, low, step)
        for i, (first, length) in enumerate(zip(firsts, lengths))
        for low in range(0, length, step)
    ]
    step_tokens = hidden.shape[0]
    return pl.pallas_call(
        functools.partial(pack_kernel, parts),
        grid_spec=pltpu.PrefetchScalarGridSpec(
            num_scalar_prefetch=1,
            grid=(1,),
            in_specs=[pl.BlockSpec(memory_space=pl.ANY)],
            out_specs=[pl.BlockSpec(memory_space=pl.ANY)] * len(firsts),
            scratch_shapes=[
                pltpu.VMEM((step_tokens, sum(lengths)), BF16),
                pltpu.SemaphoreType.DMA((2, len(parts))),
            ],
        ),
        out_shape=[pltpu.HBM((step_tokens, n), BF16) for n in lengths],
        compiler_params=pltpu.CompilerParams(vmem_limit_bytes=10 * MIB),
        cost_estimate=COST,
        name="pack_hidden",
    )(idx, *in_hbm(hidden))


def gw_kernel(npieces, low, block, idx_ref, hidden_hbm, diag_ref, swapped_ref, *refs):
    pieces = refs[:npieces]
    grads_hbm = refs[npieces]
    out_hbm, own, grads, out, in_sems, out_sems = refs[-6:]
    length = own.shape[1]
    units = out_hbm.shape[0]
    steps = length // 2 // block
    row, core = idx_ref[0], idx_ref[1]

    def columns(i):
        half = core if i < steps else 1 - core
        return pl.ds(pl.multiple_of((half * steps + i % steps) * block, block), block)

    source = pl.ds(pl.multiple_of(row * units + low, block), length)
    arriving = [
        pltpu.make_async_copy(hidden_hbm.at[:, source], own, in_sems.at[0]),
        pltpu.make_async_copy(grads_hbm, grads, in_sems.at[1]),
    ]
    for copy in arriving:
        copy.start()
    for copy in arriving:
        copy.wait()
    leaving = []
    for i in range(2 * steps):
        from_last = diag_ref if i < steps else swapped_ref
        at = (i % steps) * block
        lhs = [own[:, columns(i)], from_last[:, at : at + block]]
        lhs = jnp.concatenate(lhs + [x[:, columns(i)] for x in pieces], axis=0)
        out[i] = lax.dot_general(
            lhs, grads[...], (((0,), (0,)), ((), ())), preferred_element_type=F32
        ).astype(BF16)
        to = columns(i)
        to = pl.ds(pl.multiple_of(low + to.start, block), block)
        leaving.append(pltpu.make_async_copy(out.at[i], out_hbm.at[to, :], out_sems.at[i]))
        leaving[-1].start()
    for copy in leaving:
        copy.wait()


def gw_call(idx, hidden, diag, swapped, pieces, grads, prev, low, units):
    tokens, width = grads.shape
    step_tokens, half = diag.shape
    block = units // GW_BLOCKS
    count = 2 * half // block
    in_specs = [pl.BlockSpec(memory_space=pl.ANY)]
    in_specs += [pl.BlockSpec(memory_space=pltpu.VMEM)] * (2 + len(pieces))
    in_specs += [pl.BlockSpec(memory_space=pl.ANY)]
    args = [*in_hbm(hidden), diag, swapped, *pieces, *in_hbm(grads)]
    aliases = {}
    if prev is not None:
        in_specs += [pl.BlockSpec(memory_space=pl.ANY)]
        args += [prev]
        aliases = {len(args): 0}
    return pl.pallas_call(
        functools.partial(gw_kernel, len(pieces), low, block),
        grid_spec=pltpu.PrefetchScalarGridSpec(
            num_scalar_prefetch=1,
            grid=(1,),
            in_specs=in_specs,
            out_specs=pl.BlockSpec(memory_space=pl.ANY),
            scratch_shapes=[
                pltpu.VMEM((step_tokens, 2 * half), BF16),
                pltpu.VMEM((tokens, width), BF16),
                pltpu.VMEM((count, block, width), BF16),
                pltpu.SemaphoreType.DMA((2,)),
                pltpu.SemaphoreType.DMA((count,)),
            ],
        ),
        out_shape=pltpu.HBM((units, width), BF16),
        input_output_aliases=aliases,
        compiler_params=pltpu.CompilerParams(vmem_limit_bytes=28 * MIB),
        cost_estimate=COST,
        name="weight_gradient",
    )(idx, *args)


def gi_kernel(own_ref, *refs):
    recv = refs[:-2]
    compress_ref, out_ref = refs[-2:]
    total = own_ref[...]
    for piece in recv:
        total = total + piece[...].astype(F32)
    low = total.astype(BF16)
    blk, sub = compress_ref.shape
    for n in range(low.shape[1] // sub):
        out_ref[:, n * blk : (n + 1) * blk] = lax.dot_general(
            low[:, n * sub : (n + 1) * sub],
            compress_ref[...],
            (((1,), (1,)), ((), ())),
            preferred_element_type=F32,
        ).astype(BF16)


def gi_call(own, recv, compress, units):
    tokens, codes = own.shape
    blk, sub = compress.shape
    nblocks = codes // sub
    per = nblocks // 3 if nblocks % 3 == 0 else 1
    spec = pl.BlockSpec((tokens, per * sub), lambda j: (0, j))
    return pl.pallas_call(
        gi_kernel,
        grid=(nblocks // per,),
        in_specs=[spec] * (1 + len(recv)) + [pl.BlockSpec((blk, sub), lambda j: (0, 0))],
        out_specs=pl.BlockSpec((tokens, per * blk), lambda j: (0, j)),
        out_shape=pltpu.HBM((tokens, units), BF16),
        compiler_params=pltpu.CompilerParams(vmem_limit_bytes=10 * MIB),
        cost_estimate=LONG,
        name="grad_input",
    )(own, *recv, compress)


def on_device(nrow, ncol, out_grad, hidden, weight, compress, feedback):
    row = lax.axis_index("row")
    col = lax.axis_index("col")
    core = col % 2
    units = weight.shape[0]
    step_tokens = out_grad.shape[0]
    after = lax.optimization_barrier

    def over_row(x, k):
        return lax.ppermute(x, "row", xor_perm(nrow, k))

    def over_col(x, k):
        return lax.ppermute(x, "col", xor_perm(ncol, k))

    idx = jnp.stack([row, core, col // 2]).astype(jnp.int32)
    grads = [out_grad] + [over_row(out_grad, k) for k in range(1, nrow)]

    def joint_perm(k):
        return [
            (r * ncol + c, (r ^ (k + c % 2)) * ncol + c) for r in range(nrow) for c in range(ncol)
        ]

    pairs = range(1, nrow - 1, 2)
    lows, lengths = [0, units // 2], [units // 2] * 2
    firsts, sizes = [], []
    for low, length in zip(lows, lengths):
        firsts += [lambda r, e, k=k, low=low: (r ^ (k + e)) * units + low for k in pairs]
        firsts += [
            lambda r, e, low=low, half=length // 2: (r ^ (nrow - 1)) * units + low + e * half
        ]
        sizes += [length] * len(pairs) + [length // 2]
    packed = pack_call(idx, hidden, firsts, sizes)

    def fetch(parts):
        fetched = [lax.ppermute(x, ("row", "col"), joint_perm(k)) for k, x in zip(pairs, parts)]
        return fetched + [over_row(parts[-1], nrow - 1)]

    def swap(parts):
        swapped = [over_col(x, 1) for x in parts]
        return parts[-1], swapped[-1], [x for pair in zip(parts[:-1], swapped[:-1]) for x in pair]

    packed, grads[1:-1] = after((list(packed), grads[1:-1]))
    early = fetch(packed[: len(pairs) + 1])
    new_feedback, *codes, ordered = compress_call(idx, grads, weight, feedback, compress, ncol)
    late = fetch(packed[len(pairs) + 1 :])

    *others, kept, send = after((*early, *[over_col(x, 1) for x in codes[2:]]))
    early = swap(others)
    kept, send = [x.astype(F32) + y.astype(F32) for x, y in zip(codes[:2], (kept, send))]
    step = 1
    while True:
        received = over_col(send.astype(BF16), 2 * step)
        step *= 2
        if step == ncol // 2:
            break
        size = kept.shape[0] // 2
        send = kept[size:] + received[size:].astype(F32)
        kept = kept[:size] + received[:size].astype(F32)

    grad_weight = gw_call(idx, hidden, *early, ordered, None, lows[0], units)
    grad_weight, kept, *late = after((grad_weight, kept, *late))
    grad_input = gi_call(kept, [received], compress, units)
    diag, swapped, pieces = swap(late)
    grad_input, swapped, *pieces = after((grad_input, swapped, *pieces))
    grad_weight = gw_call(idx, hidden, diag, swapped, pieces, ordered, grad_weight, lows[1], units)
    return (grad_input, grad_weight, new_feedback)


def solution(mesh):
    return jax.shard_map(
        functools.partial(on_device, mesh.shape["row"], mesh.shape["col"]),
        mesh=mesh,
        in_specs=(P("row", "col"), P("row", None), P("row", "col"), P(), P("col", None, "row")),
        out_specs=(P("col", "row"), P("row", "col"), P("col", None, "row")),
        check_vma=False,
    )
```

```python
import functools

import jax
import jax.numpy as jnp
from jax import lax
from jax.experimental import pallas as pl
from jax.experimental.pallas import tpu as pltpu
from jax.sharding import PartitionSpec as P

F32 = jnp.float32
BF16 = jnp.bfloat16
MIB = 1024 * 1024
GW_BLOCKS = 12
LONG = pl.CostEstimate(flops=1 << 36, bytes_accessed=1 << 28, transcendentals=0)
COST = pl.CostEstimate(flops=1, bytes_accessed=1, transcendentals=0)


def in_hbm(*arrays):
    return [pltpu.with_memory_space_constraint(x, pltpu.HBM) for x in arrays]


def xor_perm(n, k):
    return [(i, i ^ k) for i in range(n)]


def place(i, count):
    bits = count.bit_length() - 1
    return sum(((i >> b) & 1) << (bits - 1 - b) for b in range(bits))


def compress_kernel(nrow, ncol, idx_ref, *refs):
    pieces = refs[:nrow]
    weight_ref, feedback_ref, compress_ref = refs[nrow : nrow + 3]
    fresh_ref, *code_refs, ordered_ref, grads, acc_buf, code_buf, sems = refs[nrow + 3 :]
    row, core = idx_ref[0], idx_ref[1]
    step_tokens = pieces[0].shape[0]
    blk, sub = compress_ref.shape
    count = weight_ref.shape[0] // blk

    def rows_at(i):
        return pl.ds(pl.multiple_of(i * step_tokens, step_tokens), step_tokens)

    def slot(k):
        if k == 0:
            return 0
        if k == nrow - 1:
            return 1
        return k + 1 + core if k % 2 else k - core + 1

    passed = [
        pltpu.make_async_copy(pieces[k], ordered_ref.at[rows_at(slot(k)), :], sems.at[k])
        for k in range(nrow)
    ]

    @pl.when(pl.program_id(0) == 0)
    def _():
        for copy in passed:
            copy.start()
        for k in range(nrow):
            grads[rows_at(row ^ k), :] = pieces[k][...]

    tokens = grads.shape[0]

    def product(b, part):
        cols = slice(part * blk // 2, (part + 1) * blk // 2)
        units = slice(b * blk + cols.start, b * blk + cols.stop)
        partial = lax.dot_general(
            grads[...], weight_ref[units, :], (((1,), (1,)), ((), ())), preferred_element_type=F32
        )
        acc_buf[b, :, cols] = partial + feedback_ref[0, :, units].astype(F32)

    def finish(b, part):
        rows = slice(part * tokens // 2, (part + 1) * tokens // 2)
        acc = acc_buf[b, rows]
        code = jnp.dot(acc.astype(BF16), compress_ref[...], preferred_element_type=F32)
        code_low = code.astype(BF16)
        code_buf[rows, b * sub : (b + 1) * sub] = code_low
        recon = lax.dot_general(
            code_low, compress_ref[...], (((1,), (1,)), ((), ())), preferred_element_type=F32
        )
        fresh_ref[0, rows, b * blk : (b + 1) * blk] = (acc - recon).astype(BF16)

    for b in range(count + 1):
        for part in range(2):
            if b < count:
                product(b, part)
            if b:
                finish(b - 1, part)

    mine_tokens = grads.shape[0] // ncol
    width = count * sub
    cols = pl.ds(pl.multiple_of(pl.program_id(0) * width, width), width)
    for i in range(ncol // 2):
        which, to = divmod(place(i, ncol // 2), ncol // 4)
        z = idx_ref[2] ^ i
        for whose, refs_of in ((core, code_refs[:2]), (1 - core, code_refs[2:])):
            at = pl.multiple_of((2 * z + whose) * mine_tokens, mine_tokens)
            refs_of[which][to * mine_tokens : (to + 1) * mine_tokens, cols] = code_buf[
                pl.ds(at, mine_tokens), :
            ]

    @pl.when(pl.program_id(0) == pl.num_programs(0) - 1)
    def _():
        for copy in passed:
            copy.wait()


def compress_call(idx, pieces, weight, feedback, compress, ncol):
    nrow = len(pieces)
    units, width = weight.shape
    blk, sub = compress.shape
    tokens = feedback.shape[1]
    nblocks = units // blk
    quarter = tokens // 4
    per = 3 if nblocks % 3 == 0 else 1
    return pl.pallas_call(
        functools.partial(compress_kernel, nrow, ncol),
        grid_spec=pltpu.PrefetchScalarGridSpec(
            num_scalar_prefetch=1,
            grid=(nblocks // per,),
            in_specs=[pl.BlockSpec((tokens // nrow, width), lambda j, s: (0, 0))]
            + [pl.BlockSpec(memory_space=pltpu.VMEM)] * (nrow - 1)
            + [
                pl.BlockSpec((per * blk, width), lambda j, s: (j, 0)),
                pl.BlockSpec((1, tokens, per * blk), lambda j, s: (0, 0, j)),
                pl.BlockSpec((blk, sub), lambda j, s: (0, 0)),
            ],
            out_specs=[pl.BlockSpec((1, tokens, per * blk), lambda j, s: (0, 0, j))]
            + [pl.BlockSpec(memory_space=pltpu.VMEM)] * 4
            + [pl.BlockSpec(memory_space=pl.ANY)],
            scratch_shapes=[
                pltpu.VMEM((tokens, width), BF16),
                pltpu.VMEM((per, tokens, blk), F32),
                pltpu.VMEM((tokens, per * sub), BF16),
                pltpu.SemaphoreType.DMA((nrow,)),
            ],
        ),
        out_shape=[pltpu.HBM((1, tokens, units), BF16)]
        + [jax.ShapeDtypeStruct((quarter, nblocks * sub), BF16)] * 4
        + [pltpu.HBM((tokens, width), BF16)],
        compiler_params=pltpu.CompilerParams(vmem_limit_bytes=30 * MIB),
        cost_estimate=LONG,
        name="compress_codes",
    )(idx, *in_hbm(pieces[0]), *pieces[1:], *in_hbm(weight, feedback, compress))


def pack_kernel(parts, idx_ref, hidden_ref, *refs):
    outs, (buf, sems) = refs[:-2], refs[-2:]
    arriving, leaving = [], []
    at = 0
    for i, (out, first, low, length) in enumerate(parts):
        source = pl.ds(pl.multiple_of(first(idx_ref[0], idx_ref[1]) + low, 128), length)
        held = buf.at[:, at : at + length]
        arriving.append(pltpu.make_async_copy(hidden_ref.at[:, source], held, sems.at[0, i]))
        leaving.append(
            pltpu.make_async_copy(held, outs[out].at[:, low : low + length], sems.at[1, i])
        )
        at += length
    for copy in arriving:
        copy.start()
    for copy, then in zip(arriving, leaving):
        copy.wait()
        then.start()
    for copy in leaving:
        copy.wait()


def pack_call(idx, hidden, firsts, lengths):
    step = min(lengths)
    parts = [
        (i, first, low, step)
        for i, (first, length) in enumerate(zip(firsts, lengths))
        for low in range(0, length, step)
    ]
    step_tokens = hidden.shape[0]
    return pl.pallas_call(
        functools.partial(pack_kernel, parts),
        grid_spec=pltpu.PrefetchScalarGridSpec(
            num_scalar_prefetch=1,
            grid=(1,),
            in_specs=[pl.BlockSpec(memory_space=pl.ANY)],
            out_specs=[pl.BlockSpec(memory_space=pl.ANY)] * len(firsts),
            scratch_shapes=[
                pltpu.VMEM((step_tokens, sum(lengths)), BF16),
                pltpu.SemaphoreType.DMA((2, len(parts))),
            ],
        ),
        out_shape=[pltpu.HBM((step_tokens, n), BF16) for n in lengths],
        compiler_params=pltpu.CompilerParams(vmem_limit_bytes=10 * MIB),
        cost_estimate=COST,
        name="pack_hidden",
    )(idx, *in_hbm(hidden))


def gw_kernel(npieces, low, block, idx_ref, hidden_hbm, diag_ref, swapped_ref, *refs):
    pieces = refs[:npieces]
    grads_hbm = refs[npieces]
    out_hbm, own, grads, out, in_sems, out_sems = refs[-6:]
    length = own.shape[1]
    units = out_hbm.shape[0]
    steps = length // 2 // block
    row, core = idx_ref[0], idx_ref[1]

    def columns(i):
        half = core if i < steps else 1 - core
        return pl.ds(pl.multiple_of((half * steps + i % steps) * block, block), block)

    source = pl.ds(pl.multiple_of(row * units + low, block), length)
    arriving = [
        pltpu.make_async_copy(hidden_hbm.at[:, source], own, in_sems.at[0]),
        pltpu.make_async_copy(grads_hbm, grads, in_sems.at[1]),
    ]
    for copy in arriving:
        copy.start()
    for copy in arriving:
        copy.wait()
    leaving = []
    for i in range(2 * steps):
        from_last = diag_ref if i < steps else swapped_ref
        at = (i % steps) * block
        lhs = [own[:, columns(i)], from_last[:, at : at + block]]
        lhs = jnp.concatenate(lhs + [x[:, columns(i)] for x in pieces], axis=0)
        out[i] = lax.dot_general(
            lhs, grads[...], (((0,), (0,)), ((), ())), preferred_element_type=F32
        ).astype(BF16)
        to = columns(i)
        to = pl.ds(pl.multiple_of(low + to.start, block), block)
        leaving.append(pltpu.make_async_copy(out.at[i], out_hbm.at[to, :], out_sems.at[i]))
        leaving[-1].start()
    for copy in leaving:
        copy.wait()


def gw_call(idx, hidden, diag, swapped, pieces, grads, prev, low, units):
    tokens, width = grads.shape
    step_tokens, half = diag.shape
    block = units // GW_BLOCKS
    count = 2 * half // block
    in_specs = [pl.BlockSpec(memory_space=pl.ANY)]
    in_specs += [pl.BlockSpec(memory_space=pltpu.VMEM)] * (2 + len(pieces))
    in_specs += [pl.BlockSpec(memory_space=pl.ANY)]
    args = [*in_hbm(hidden), diag, swapped, *pieces, *in_hbm(grads)]
    aliases = {}
    if prev is not None:
        in_specs += [pl.BlockSpec(memory_space=pl.ANY)]
        args += [prev]
        aliases = {len(args): 0}
    return pl.pallas_call(
        functools.partial(gw_kernel, len(pieces), low, block),
        grid_spec=pltpu.PrefetchScalarGridSpec(
            num_scalar_prefetch=1,
            grid=(1,),
            in_specs=in_specs,
            out_specs=pl.BlockSpec(memory_space=pl.ANY),
            scratch_shapes=[
                pltpu.VMEM((step_tokens, 2 * half), BF16),
                pltpu.VMEM((tokens, width), BF16),
                pltpu.VMEM((count, block, width), BF16),
                pltpu.SemaphoreType.DMA((2,)),
                pltpu.SemaphoreType.DMA((count,)),
            ],
        ),
        out_shape=pltpu.HBM((units, width), BF16),
        input_output_aliases=aliases,
        compiler_params=pltpu.CompilerParams(vmem_limit_bytes=28 * MIB),
        cost_estimate=COST,
        name="weight_gradient",
    )(idx, *args)


def gi_kernel(parts, *refs):
    compress_ref, out_ref = refs[-2:]
    blk, sub = compress_ref.shape
    at = 0
    for own, received in zip(refs[:parts], refs[parts : 2 * parts]):
        low = (own[...] + received[...].astype(F32)).astype(BF16)
        for n in range(low.shape[1] // sub):
            out_ref[:, at : at + blk] = lax.dot_general(
                low[:, n * sub : (n + 1) * sub],
                compress_ref[...],
                (((1,), (1,)), ((), ())),
                preferred_element_type=F32,
            ).astype(BF16)
            at += blk


def gi_call(own, received, compress, units):
    tokens = own[0].shape[0]
    return pl.pallas_call(
        functools.partial(gi_kernel, len(own)),
        in_specs=[pl.BlockSpec(memory_space=pltpu.VMEM)] * (2 * len(own) + 1),
        out_specs=pl.BlockSpec(memory_space=pltpu.VMEM),
        out_shape=jax.ShapeDtypeStruct((tokens, units), BF16),
        compiler_params=pltpu.CompilerParams(vmem_limit_bytes=10 * MIB),
        cost_estimate=LONG,
        name="grad_input",
    )(*own, *received, compress)


def on_device(nrow, ncol, out_grad, hidden, weight, compress, feedback):
    row = lax.axis_index("row")
    col = lax.axis_index("col")
    core = col % 2
    units = weight.shape[0]
    step_tokens = out_grad.shape[0]
    after = lax.optimization_barrier

    def over_row(x, k):
        return lax.ppermute(x, "row", xor_perm(nrow, k))

    def over_col(x, k):
        return lax.ppermute(x, "col", xor_perm(ncol, k))

    idx = jnp.stack([row, core, col // 2]).astype(jnp.int32)
    grads = [out_grad] + [over_row(out_grad, k) for k in range(1, nrow)]

    def joint_perm(k):
        return [
            (r * ncol + c, (r ^ (k + c % 2)) * ncol + c) for r in range(nrow) for c in range(ncol)
        ]

    pairs = range(1, nrow - 1, 2)
    lows, lengths = [0, units // 2], [units // 2] * 2
    firsts, sizes = [], []
    for low, length in zip(lows, lengths):
        firsts += [lambda r, e, k=k, low=low: (r ^ (k + e)) * units + low for k in pairs]
        firsts += [
            lambda r, e, low=low, half=length // 2: (r ^ (nrow - 1)) * units + low + e * half
        ]
        sizes += [length] * len(pairs) + [length // 2]
    packed = pack_call(idx, hidden, firsts, sizes)

    def fetch(parts):
        fetched = [lax.ppermute(x, ("row", "col"), joint_perm(k)) for k, x in zip(pairs, parts)]
        return fetched + [over_row(parts[-1], nrow - 1)]

    def swap(parts):
        swapped = [over_col(x, 1) for x in parts]
        return parts[-1], swapped[-1], [x for pair in zip(parts[:-1], swapped[:-1]) for x in pair]

    early = fetch(packed[: len(pairs) + 1])
    new_feedback, *codes, ordered = compress_call(idx, grads, weight, feedback, compress, ncol)
    late = fetch(packed[len(pairs) + 1 :])

    *others, kept, send = after((*early, *[over_col(x, 1) for x in codes[2:]]))
    early = list(swap(others))
    kept, send = [x.astype(F32) + y.astype(F32) for x, y in zip(codes[:2], (kept, send))]
    step = 1
    while True:
        received = over_col(send.astype(BF16), 2 * step)
        step *= 2
        if step == ncol // 2:
            break
        size = kept.shape[0] // 2
        send = kept[size:] + received[size:].astype(F32)
        kept = kept[:size] + received[:size].astype(F32)

    grad_weight = gw_call(idx, hidden, *early, ordered, None, lows[0], units)
    grad_weight, kept, *late = after((grad_weight, kept, *late))
    grad_input = gi_call([kept], [received], compress, units)
    diag, swapped, pieces = swap(late)
    grad_input, swapped, *pieces = after((grad_input, swapped, *pieces))
    grad_weight = gw_call(idx, hidden, diag, swapped, pieces, ordered, grad_weight, lows[1], units)
    return (grad_input, grad_weight, new_feedback)


def solution(mesh):
    return jax.shard_map(
        functools.partial(on_device, mesh.shape["row"], mesh.shape["col"]),
        mesh=mesh,
        in_specs=(P("row", "col"), P("row", None), P("row", "col"), P(), P("col", None, "row")),
        out_specs=(P("col", "row"), P("row", "col"), P("col", None, "row")),
        check_vma=False,
    )
```

```python
import functools

import jax
import jax.numpy as jnp
from jax import lax
from jax.experimental import pallas as pl
from jax.experimental.pallas import tpu as pltpu
from jax.sharding import PartitionSpec as P

F32 = jnp.float32
BF16 = jnp.bfloat16
MIB = 1024 * 1024
GW_BLOCKS = 8
LONG = pl.CostEstimate(flops=1 << 36, bytes_accessed=1 << 28, transcendentals=0)
COST = pl.CostEstimate(flops=1, bytes_accessed=1, transcendentals=0)


def in_hbm(*arrays):
    return [pltpu.with_memory_space_constraint(x, pltpu.HBM) for x in arrays]


def xor_perm(n, k):
    return [(i, i ^ k) for i in range(n)]


def place(i, count):
    bits = count.bit_length() - 1
    return sum(((i >> b) & 1) << (bits - 1 - b) for b in range(bits))


def compress_kernel(nrow, ncol, idx_ref, *refs):
    pieces = refs[:nrow]
    weight_ref, feedback_ref, compress_ref = refs[nrow : nrow + 3]
    fresh_ref, *code_refs, ordered_ref, grads, acc_buf, code_buf, sems = refs[nrow + 3 :]
    row, core = idx_ref[0], idx_ref[1]
    step_tokens = pieces[0].shape[0]
    blk, sub = compress_ref.shape
    count = weight_ref.shape[0] // blk

    def rows_at(i):
        return pl.ds(pl.multiple_of(i * step_tokens, step_tokens), step_tokens)

    def slot(k):
        if k == 0:
            return 0
        if k == nrow - 1:
            return 1
        return k + 1 + core if k % 2 else k - core + 1

    passed = [
        pltpu.make_async_copy(pieces[k], ordered_ref.at[rows_at(slot(k)), :], sems.at[k])
        for k in range(nrow)
    ]

    @pl.when(pl.program_id(0) == 0)
    def _():
        for copy in passed:
            copy.start()
        for k in range(nrow):
            grads[rows_at(row ^ k), :] = pieces[k][...]

    def product(b):
        cols = slice(b * blk, (b + 1) * blk)
        partial = lax.dot_general(
            grads[...], weight_ref[cols, :], (((1,), (1,)), ((), ())), preferred_element_type=F32
        )
        acc_buf[b] = partial + feedback_ref[0, :, cols].astype(F32)

    def finish(b):
        acc = acc_buf[b]
        code = jnp.dot(acc.astype(BF16), compress_ref[...], preferred_element_type=F32)
        code_low = code.astype(BF16)
        code_buf[:, b * sub : (b + 1) * sub] = code_low
        recon = lax.dot_general(
            code_low, compress_ref[...], (((1,), (1,)), ((), ())), preferred_element_type=F32
        )
        fresh_ref[0, :, b * blk : (b + 1) * blk] = (acc - recon).astype(BF16)

    for b in range(count):
        product(b)
        if b:
            finish(b - 1)
    finish(count - 1)

    mine_tokens = grads.shape[0] // ncol
    width = count * sub
    cols = pl.ds(pl.multiple_of(pl.program_id(0) * width, width), width)
    for i in range(ncol // 2):
        which, to = divmod(place(i, ncol // 2), ncol // 4)
        z = idx_ref[2] ^ i
        for whose, refs_of in ((core, code_refs[:2]), (1 - core, code_refs[2:])):
            at = pl.multiple_of((2 * z + whose) * mine_tokens, mine_tokens)
            refs_of[which][to * mine_tokens : (to + 1) * mine_tokens, cols] = code_buf[
                pl.ds(at, mine_tokens), :
            ]

    @pl.when(pl.program_id(0) == pl.num_programs(0) - 1)
    def _():
        for copy in passed:
            copy.wait()


def compress_call(idx, pieces, weight, feedback, compress, ncol):
    nrow = len(pieces)
    units, width = weight.shape
    blk, sub = compress.shape
    tokens = feedback.shape[1]
    nblocks = units // blk
    quarter = tokens // 4
    per = next(n for n in (4, 3, 2, 1) if nblocks % n == 0)
    return pl.pallas_call(
        functools.partial(compress_kernel, nrow, ncol),
        grid_spec=pltpu.PrefetchScalarGridSpec(
            num_scalar_prefetch=1,
            grid=(nblocks // per,),
            in_specs=[pl.BlockSpec((tokens // nrow, width), lambda j, s: (0, 0))]
            + [pl.BlockSpec(memory_space=pltpu.VMEM)] * (nrow - 1)
            + [
                pl.BlockSpec((per * blk, width), lambda j, s: (j, 0)),
                pl.BlockSpec((1, tokens, per * blk), lambda j, s: (0, 0, j)),
                pl.BlockSpec((blk, sub), lambda j, s: (0, 0)),
            ],
            out_specs=[pl.BlockSpec((1, tokens, per * blk), lambda j, s: (0, 0, j))]
            + [pl.BlockSpec(memory_space=pltpu.VMEM)] * 4
            + [pl.BlockSpec(memory_space=pl.ANY)],
            scratch_shapes=[
                pltpu.VMEM((tokens, width), BF16),
                pltpu.VMEM((per, tokens, blk), F32),
                pltpu.VMEM((tokens, per * sub), BF16),
                pltpu.SemaphoreType.DMA((nrow,)),
            ],
        ),
        out_shape=[pltpu.HBM((1, tokens, units), BF16)]
        + [jax.ShapeDtypeStruct((quarter, nblocks * sub), BF16)] * 4
        + [pltpu.HBM((tokens, width), BF16)],
        compiler_params=pltpu.CompilerParams(vmem_limit_bytes=30 * MIB),
        cost_estimate=LONG,
        name="compress_codes",
    )(idx, *in_hbm(pieces[0]), *pieces[1:], *in_hbm(weight, feedback, compress))


def pack_kernel(parts, idx_ref, hidden_ref, *refs):
    outs, (buf, sems) = refs[:-2], refs[-2:]
    arriving, leaving = [], []
    at = 0
    for i, (out, first, low, length) in enumerate(parts):
        source = pl.ds(pl.multiple_of(first(idx_ref[0], idx_ref[1]) + low, 128), length)
        held = buf.at[:, at : at + length]
        arriving.append(pltpu.make_async_copy(hidden_ref.at[:, source], held, sems.at[0, i]))
        leaving.append(
            pltpu.make_async_copy(held, outs[out].at[:, low : low + length], sems.at[1, i])
        )
        at += length
    for copy in arriving:
        copy.start()
    for copy, then in zip(arriving, leaving):
        copy.wait()
        then.start()
    for copy in leaving:
        copy.wait()


def pack_call(idx, hidden, firsts, lengths):
    step = min(lengths)
    parts = [
        (i, first, low, step)
        for i, (first, length) in enumerate(zip(firsts, lengths))
        for low in range(0, length, step)
    ]
    step_tokens = hidden.shape[0]
    return pl.pallas_call(
        functools.partial(pack_kernel, parts),
        grid_spec=pltpu.PrefetchScalarGridSpec(
            num_scalar_prefetch=1,
            grid=(1,),
            in_specs=[pl.BlockSpec(memory_space=pl.ANY)],
            out_specs=[pl.BlockSpec(memory_space=pl.ANY)] * len(firsts),
            scratch_shapes=[
                pltpu.VMEM((step_tokens, sum(lengths)), BF16),
                pltpu.SemaphoreType.DMA((2, len(parts))),
            ],
        ),
        out_shape=[pltpu.HBM((step_tokens, n), BF16) for n in lengths],
        compiler_params=pltpu.CompilerParams(vmem_limit_bytes=10 * MIB),
        cost_estimate=COST,
        name="pack_hidden",
    )(idx, *in_hbm(hidden))


def gw_blocks(core, low, block, own, diag, swapped, pieces, grads, out, out_hbm, sems):
    steps = diag.shape[1] // block

    def columns(i):
        half = core if i < steps else 1 - core
        return pl.ds(pl.multiple_of((half * steps + i % steps) * block, block), block)

    leaving = []
    for i in range(2 * steps):
        from_last = diag if i < steps else swapped
        at = (i % steps) * block
        lhs = [own[:, columns(i)], from_last[:, at : at + block]]
        lhs = jnp.concatenate(lhs + [x[:, columns(i)] for x in pieces], axis=0)
        out[i] = lax.dot_general(
            lhs, grads[...], (((0,), (0,)), ((), ())), preferred_element_type=F32
        ).astype(BF16)
        to = pl.ds(pl.multiple_of(low + columns(i).start, block), block)
        leaving.append(pltpu.make_async_copy(out.at[i], out_hbm.at[to, :], sems.at[i]))
        leaving[-1].start()
    for copy in leaving:
        copy.wait()


def gw_first_kernel(npieces, lows, block, idx_ref, hidden_hbm, diag, swapped, *refs):
    pieces = refs[:npieces]
    grads_hbm, out_hbm, own_next, grads, own, out, in_sems, out_sems = refs[npieces:]
    units = out_hbm.shape[0]
    row, core = idx_ref[0], idx_ref[1]

    def arriving(i, to):
        source = pl.ds(pl.multiple_of(row * units + lows[i], block), to.shape[1])
        return pltpu.make_async_copy(hidden_hbm.at[:, source], to, in_sems.at[i])

    copies = [
        arriving(0, own),
        pltpu.make_async_copy(grads_hbm, grads, in_sems.at[2]),
        arriving(1, own_next),
    ]
    for copy in copies:
        copy.start()
    for copy in copies:
        copy.wait()
    gw_blocks(core, lows[0], block, own, diag, swapped, pieces, grads, out, out_hbm, out_sems)


def gw_last_kernel(npieces, low, block, idx_ref, own, diag, swapped, *refs):
    pieces = refs[:npieces]
    grads, _, out_hbm, out, sems = refs[npieces:]
    gw_blocks(idx_ref[1], low, block, own, diag, swapped, pieces, grads, out, out_hbm, sems)


def gw_call(kernel, idx, args, spaces, count, block, outs, scratch, aliases):
    width = outs[0].shape[1]
    return pl.pallas_call(
        kernel,
        grid_spec=pltpu.PrefetchScalarGridSpec(
            num_scalar_prefetch=1,
            grid=(1,),
            in_specs=[pl.BlockSpec(memory_space=space) for space in spaces],
            out_specs=[pl.BlockSpec(memory_space=pl.ANY)]
            + [pl.BlockSpec(memory_space=pltpu.VMEM)] * (len(outs) - 1),
            scratch_shapes=[
                *scratch,
                pltpu.VMEM((count, block, width), BF16),
                *([pltpu.SemaphoreType.DMA((3,))] if scratch else []),
                pltpu.SemaphoreType.DMA((count,)),
            ],
        ),
        out_shape=outs,
        input_output_aliases=aliases,
        compiler_params=pltpu.CompilerParams(vmem_limit_bytes=28 * MIB),
        cost_estimate=COST,
        name="weight_gradient",
    )(idx, *args)


def gw_first(idx, hidden, diag, swapped, pieces, grads, lows, units):
    tokens, width = grads.shape
    step_tokens, half = diag.shape
    block = units // GW_BLOCKS
    return gw_call(
        functools.partial(gw_first_kernel, len(pieces), lows, block),
        idx,
        [*in_hbm(hidden), diag, swapped, *pieces, *in_hbm(grads)],
        [pl.ANY] + [pltpu.VMEM] * (2 + len(pieces)) + [pl.ANY],
        2 * half // block,
        block,
        [
            pltpu.HBM((units, width), BF16),
            jax.ShapeDtypeStruct((step_tokens, units - lows[1]), BF16),
            jax.ShapeDtypeStruct((tokens, width), BF16),
        ],
        [pltpu.VMEM((step_tokens, 2 * half), BF16)],
        {},
    )


def gw_last(idx, own, diag, swapped, pieces, grads, prev, low):
    block = prev.shape[0] // GW_BLOCKS
    args = [own, diag, swapped, *pieces, grads, prev]
    (grad_weight,) = gw_call(
        functools.partial(gw_last_kernel, len(pieces), low, block),
        idx,
        args,
        [pltpu.VMEM] * (len(args) - 1) + [pl.ANY],
        2 * diag.shape[1] // block,
        block,
        [pltpu.HBM(prev.shape, BF16)],
        [],
        {len(args): 0},
    )
    return grad_weight


def gi_kernel(parts, *refs):
    compress_ref, out_ref = refs[-2:]
    blk, sub = compress_ref.shape
    at = 0
    for own, received in zip(refs[:parts], refs[parts : 2 * parts]):
        low = (own[...] + received[...].astype(F32)).astype(BF16)
        for n in range(low.shape[1] // sub):
            out_ref[:, at : at + blk] = lax.dot_general(
                low[:, n * sub : (n + 1) * sub],
                compress_ref[...],
                (((1,), (1,)), ((), ())),
                preferred_element_type=F32,
            ).astype(BF16)
            at += blk


def gi_call(own, received, compress, units):
    tokens = own[0].shape[0]
    return pl.pallas_call(
        functools.partial(gi_kernel, len(own)),
        in_specs=[pl.BlockSpec(memory_space=pltpu.VMEM)] * (2 * len(own) + 1),
        out_specs=pl.BlockSpec(memory_space=pltpu.VMEM),
        out_shape=jax.ShapeDtypeStruct((tokens, units), BF16),
        compiler_params=pltpu.CompilerParams(vmem_limit_bytes=10 * MIB),
        cost_estimate=LONG,
        name="grad_input",
    )(*own, *received, compress)


def on_device(nrow, ncol, out_grad, hidden, weight, compress, feedback):
    row = lax.axis_index("row")
    col = lax.axis_index("col")
    core = col % 2
    units = weight.shape[0]
    step_tokens = out_grad.shape[0]
    after = lax.optimization_barrier

    def over_row(x, k):
        return lax.ppermute(x, "row", xor_perm(nrow, k))

    def over_col(x, k):
        return lax.ppermute(x, "col", xor_perm(ncol, k))

    idx = jnp.stack([row, core, col // 2]).astype(jnp.int32)
    grads = [out_grad] + [over_row(out_grad, k) for k in range(1, nrow)]

    def joint_perm(k):
        return [
            (r * ncol + c, (r ^ (k + c % 2)) * ncol + c) for r in range(nrow) for c in range(ncol)
        ]

    pairs = range(1, nrow - 1, 2)
    lows, lengths = [0, units // 4 * 3], [units // 4 * 3, units // 4]
    firsts, sizes = [], []
    for low, length in zip(lows, lengths):
        firsts += [lambda r, e, k=k, low=low: (r ^ (k + e)) * units + low for k in pairs]
        firsts += [
            lambda r, e, low=low, half=length // 2: (r ^ (nrow - 1)) * units + low + e * half
        ]
        sizes += [length] * len(pairs) + [length // 2]
    packed = pack_call(idx, hidden, firsts, sizes)

    def fetch(parts):
        fetched = [lax.ppermute(x, ("row", "col"), joint_perm(k)) for k, x in zip(pairs, parts)]
        return fetched + [over_row(parts[-1], nrow - 1)]

    def swap(parts):
        swapped = [over_col(x, 1) for x in parts]
        return parts[-1], swapped[-1], [x for pair in zip(parts[:-1], swapped[:-1]) for x in pair]

    early = fetch(packed[: len(pairs) + 1])
    new_feedback, *codes, ordered = compress_call(idx, grads, weight, feedback, compress, ncol)

    early[-1], kept, send = after((early[-1], *[over_col(x, 1) for x in codes[2:]]))
    *direct, packed = packed[len(pairs) + 1 :]
    packed, early[0] = after((packed, early[0]))
    early = swap(early)
    kept, send = [x.astype(F32) + y.astype(F32) for x, y in zip(codes[:2], (kept, send))]
    send, *direct = after((send.astype(BF16), *direct))
    late = fetch([*direct, packed])
    step = 1
    while True:
        received = over_col(send.astype(BF16), 2 * step)
        step *= 2
        if step == ncol // 2:
            break
        size = kept.shape[0] // 2
        send = kept[size:] + received[size:].astype(F32)
        kept = kept[:size] + received[:size].astype(F32)

    grad_weight, own, grads = gw_first(idx, hidden, *early, ordered, lows, units)
    grad_weight, kept, *late = after((grad_weight, kept, *late))
    grad_input = gi_call([kept], [received], compress, units)
    diag, swapped, pieces = swap(late)
    grad_input, swapped, *pieces = after((grad_input, swapped, *pieces))
    grad_weight = gw_last(idx, own, diag, swapped, pieces, grads, grad_weight, lows[1])
    return (grad_input, grad_weight, new_feedback)


def solution(mesh):
    return jax.shard_map(
        functools.partial(on_device, mesh.shape["row"], mesh.shape["col"]),
        mesh=mesh,
        in_specs=(P("row", "col"), P("row", None), P("row", "col"), P(), P("col", None, "row")),
        out_specs=(P("col", "row"), P("row", "col"), P("col", None, "row")),
        check_vma=False,
    )
```

```python
import functools

import jax
import jax.numpy as jnp
from jax import lax
from jax.experimental import pallas as pl
from jax.experimental.pallas import tpu as pltpu
from jax.sharding import PartitionSpec as P

F32 = jnp.float32
BF16 = jnp.bfloat16
MIB = 1024 * 1024
GW_BLOCKS = 8
LONG = pl.CostEstimate(flops=1 << 36, bytes_accessed=1 << 28, transcendentals=0)
COST = pl.CostEstimate(flops=1, bytes_accessed=1, transcendentals=0)


def in_hbm(*arrays):
    return [pltpu.with_memory_space_constraint(x, pltpu.HBM) for x in arrays]


def xor_perm(n, k):
    return [(i, i ^ k) for i in range(n)]


def place(i, count):
    bits = count.bit_length() - 1
    return sum(((i >> b) & 1) << (bits - 1 - b) for b in range(bits))


def compress_kernel(nrow, ncol, idx_ref, *refs):
    pieces = refs[:nrow]
    weight_ref, feedback_ref, compress_ref = refs[nrow : nrow + 3]
    fresh_ref, *code_refs, ordered_ref, grads, acc_buf, code_buf, sems = refs[nrow + 3 :]
    row, core = idx_ref[0], idx_ref[1]
    step_tokens = pieces[0].shape[0]
    blk, sub = compress_ref.shape
    count = weight_ref.shape[0] // blk

    def rows_at(i):
        return pl.ds(pl.multiple_of(i * step_tokens, step_tokens), step_tokens)

    def slot(k):
        if k == 0:
            return 0
        if k == nrow - 1:
            return 1
        return k + 1 + core if k % 2 else k - core + 1

    passed = [
        pltpu.make_async_copy(pieces[k], ordered_ref.at[rows_at(slot(k)), :], sems.at[k])
        for k in range(nrow)
    ]

    @pl.when(pl.program_id(0) == 0)
    def _():
        for copy in passed:
            copy.start()
        for k in range(nrow):
            grads[rows_at(row ^ k), :] = pieces[k][...]

    def product(b):
        cols = slice(b * blk, (b + 1) * blk)
        partial = lax.dot_general(
            grads[...], weight_ref[cols, :], (((1,), (1,)), ((), ())), preferred_element_type=F32
        )
        acc_buf[b] = partial + feedback_ref[0, :, cols].astype(F32)

    def finish(b):
        acc = acc_buf[b]
        code = jnp.dot(acc.astype(BF16), compress_ref[...], preferred_element_type=F32)
        code_low = code.astype(BF16)
        code_buf[:, b * sub : (b + 1) * sub] = code_low
        recon = lax.dot_general(
            code_low, compress_ref[...], (((1,), (1,)), ((), ())), preferred_element_type=F32
        )
        fresh_ref[0, :, b * blk : (b + 1) * blk] = (acc - recon).astype(BF16)

    for b in range(count):
        product(b)
        if b:
            finish(b - 1)
    finish(count - 1)

    mine_tokens = grads.shape[0] // ncol
    width = count * sub
    cols = pl.ds(pl.multiple_of(pl.program_id(0) * width, width), width)
    for i in range(ncol // 2):
        which, to = divmod(place(i, ncol // 2), ncol // 4)
        z = idx_ref[2] ^ i
        for whose, refs_of in ((core, code_refs[:2]), (1 - core, code_refs[2:])):
            at = pl.multiple_of((2 * z + whose) * mine_tokens, mine_tokens)
            refs_of[which][to * mine_tokens : (to + 1) * mine_tokens, cols] = code_buf[
                pl.ds(at, mine_tokens), :
            ]

    @pl.when(pl.program_id(0) == pl.num_programs(0) - 1)
    def _():
        for copy in passed:
            copy.wait()


def compress_call(idx, pieces, weight, feedback, compress, ncol):
    nrow = len(pieces)
    units, width = weight.shape
    blk, sub = compress.shape
    tokens = feedback.shape[1]
    nblocks = units // blk
    quarter = tokens // 4
    per = next(n for n in (4, 3, 2, 1) if nblocks % n == 0)
    return pl.pallas_call(
        functools.partial(compress_kernel, nrow, ncol),
        grid_spec=pltpu.PrefetchScalarGridSpec(
            num_scalar_prefetch=1,
            grid=(nblocks // per,),
            in_specs=[pl.BlockSpec((tokens // nrow, width), lambda j, s: (0, 0))]
            + [pl.BlockSpec(memory_space=pltpu.VMEM)] * (nrow - 1)
            + [
                pl.BlockSpec((per * blk, width), lambda j, s: (j, 0)),
                pl.BlockSpec((1, tokens, per * blk), lambda j, s: (0, 0, j)),
                pl.BlockSpec((blk, sub), lambda j, s: (0, 0)),
            ],
            out_specs=[pl.BlockSpec((1, tokens, per * blk), lambda j, s: (0, 0, j))]
            + [pl.BlockSpec(memory_space=pltpu.VMEM)] * 4
            + [pl.BlockSpec(memory_space=pl.ANY)],
            scratch_shapes=[
                pltpu.VMEM((tokens, width), BF16),
                pltpu.VMEM((per, tokens, blk), F32),
                pltpu.VMEM((tokens, per * sub), BF16),
                pltpu.SemaphoreType.DMA((nrow,)),
            ],
        ),
        out_shape=[pltpu.HBM((1, tokens, units), BF16)]
        + [jax.ShapeDtypeStruct((quarter, nblocks * sub), BF16)] * 4
        + [pltpu.HBM((tokens, width), BF16)],
        compiler_params=pltpu.CompilerParams(vmem_limit_bytes=30 * MIB),
        cost_estimate=LONG,
        name="compress_codes",
    )(idx, *in_hbm(pieces[0]), *pieces[1:], *in_hbm(weight, feedback, compress))


def pack_kernel(parts, idx_ref, hidden_ref, *refs):
    outs, (buf, sems) = refs[:-2], refs[-2:]
    arriving, leaving = [], []
    at = 0
    for i, (out, first, low, length) in enumerate(parts):
        source = pl.ds(pl.multiple_of(first(idx_ref[0], idx_ref[1]) + low, 128), length)
        held = buf.at[:, at : at + length]
        arriving.append(pltpu.make_async_copy(hidden_ref.at[:, source], held, sems.at[0, i]))
        leaving.append(
            pltpu.make_async_copy(held, outs[out].at[:, low : low + length], sems.at[1, i])
        )
        at += length
    for copy in arriving:
        copy.start()
    for copy, then in zip(arriving, leaving):
        copy.wait()
        then.start()
    for copy in leaving:
        copy.wait()


def pack_call(idx, hidden, firsts, lengths):
    step = min(lengths)
    parts = [
        (i, first, low, step)
        for i, (first, length) in enumerate(zip(firsts, lengths))
        for low in range(0, length, step)
    ]
    step_tokens = hidden.shape[0]
    return pl.pallas_call(
        functools.partial(pack_kernel, parts),
        grid_spec=pltpu.PrefetchScalarGridSpec(
            num_scalar_prefetch=1,
            grid=(1,),
            in_specs=[pl.BlockSpec(memory_space=pl.ANY)],
            out_specs=[pl.BlockSpec(memory_space=pl.ANY)] * len(firsts),
            scratch_shapes=[
                pltpu.VMEM((step_tokens, sum(lengths)), BF16),
                pltpu.SemaphoreType.DMA((2, len(parts))),
            ],
        ),
        out_shape=[pltpu.HBM((step_tokens, n), BF16) for n in lengths],
        compiler_params=pltpu.CompilerParams(vmem_limit_bytes=10 * MIB),
        cost_estimate=COST,
        name="pack_hidden",
    )(idx, *in_hbm(hidden))


def gw_blocks(core, low, block, own, diag, swapped, pieces, grads, out, out_hbm, sems):
    steps = diag.shape[1] // block

    def columns(i):
        half = core if i < steps else 1 - core
        return pl.ds(pl.multiple_of((half * steps + i % steps) * block, block), block)

    leaving = []
    for i in range(2 * steps):
        from_last = diag if i < steps else swapped
        at = (i % steps) * block
        lhs = [own[:, columns(i)], from_last[:, at : at + block]]
        lhs = jnp.concatenate(lhs + [x[:, columns(i)] for x in pieces], axis=0)
        out[i] = lax.dot_general(
            lhs, grads[...], (((0,), (0,)), ((), ())), preferred_element_type=F32
        ).astype(BF16)
        to = pl.ds(pl.multiple_of(low + columns(i).start, block), block)
        leaving.append(pltpu.make_async_copy(out.at[i], out_hbm.at[to, :], sems.at[i]))
        leaving[-1].start()
    for copy in leaving:
        copy.wait()


def gw_first_kernel(npieces, lows, block, idx_ref, hidden_hbm, diag, swapped, *refs):
    pieces = refs[:npieces]
    grads_hbm, out_hbm, own_next, grads, own, out, in_sems, out_sems = refs[npieces:]
    units = out_hbm.shape[0]
    row, core = idx_ref[0], idx_ref[1]

    def arriving(i, to):
        source = pl.ds(pl.multiple_of(row * units + lows[i], block), to.shape[1])
        return pltpu.make_async_copy(hidden_hbm.at[:, source], to, in_sems.at[i])

    copies = [
        arriving(0, own),
        pltpu.make_async_copy(grads_hbm, grads, in_sems.at[2]),
        arriving(1, own_next),
    ]
    for copy in copies:
        copy.start()
    for copy in copies:
        copy.wait()
    gw_blocks(core, lows[0], block, own, diag, swapped, pieces, grads, out, out_hbm, out_sems)


def gw_last_kernel(npieces, low, block, idx_ref, own, diag, swapped, *refs):
    pieces = refs[:npieces]
    grads, _, out_hbm, out, sems = refs[npieces:]
    gw_blocks(idx_ref[1], low, block, own, diag, swapped, pieces, grads, out, out_hbm, sems)


def gw_call(kernel, idx, args, spaces, count, block, outs, scratch, aliases):
    width = outs[0].shape[1]
    return pl.pallas_call(
        kernel,
        grid_spec=pltpu.PrefetchScalarGridSpec(
            num_scalar_prefetch=1,
            grid=(1,),
            in_specs=[pl.BlockSpec(memory_space=space) for space in spaces],
            out_specs=[pl.BlockSpec(memory_space=pl.ANY)]
            + [pl.BlockSpec(memory_space=pltpu.VMEM)] * (len(outs) - 1),
            scratch_shapes=[
                *scratch,
                pltpu.VMEM((count, block, width), BF16),
                *([pltpu.SemaphoreType.DMA((3,))] if scratch else []),
                pltpu.SemaphoreType.DMA((count,)),
            ],
        ),
        out_shape=outs,
        input_output_aliases=aliases,
        compiler_params=pltpu.CompilerParams(vmem_limit_bytes=28 * MIB),
        cost_estimate=COST,
        name="weight_gradient",
    )(idx, *args)


def gw_first(idx, hidden, diag, swapped, pieces, grads, lows, units):
    tokens, width = grads.shape
    step_tokens, half = diag.shape
    block = units // GW_BLOCKS
    return gw_call(
        functools.partial(gw_first_kernel, len(pieces), lows, block),
        idx,
        [*in_hbm(hidden), diag, swapped, *pieces, *in_hbm(grads)],
        [pl.ANY] + [pltpu.VMEM] * (2 + len(pieces)) + [pl.ANY],
        2 * half // block,
        block,
        [
            pltpu.HBM((units, width), BF16),
            jax.ShapeDtypeStruct((step_tokens, units - lows[1]), BF16),
            jax.ShapeDtypeStruct((tokens, width), BF16),
        ],
        [pltpu.VMEM((step_tokens, 2 * half), BF16)],
        {},
    )


def gw_last(idx, own, diag, swapped, pieces, grads, prev, low):
    block = prev.shape[0] // GW_BLOCKS
    args = [own, diag, swapped, *pieces, grads, prev]
    (grad_weight,) = gw_call(
        functools.partial(gw_last_kernel, len(pieces), low, block),
        idx,
        args,
        [pltpu.VMEM] * (len(args) - 1) + [pl.ANY],
        2 * diag.shape[1] // block,
        block,
        [pltpu.HBM(prev.shape, BF16)],
        [],
        {len(args): 0},
    )
    return grad_weight


def gi_kernel(parts, *refs):
    compress_ref, out_ref = refs[-2:]
    blk, sub = compress_ref.shape
    at = 0
    for own, received in zip(refs[:parts], refs[parts : 2 * parts]):
        low = (own[...] + received[...].astype(F32)).astype(BF16)
        for n in range(low.shape[1] // sub):
            out_ref[:, at : at + blk] = lax.dot_general(
                low[:, n * sub : (n + 1) * sub],
                compress_ref[...],
                (((1,), (1,)), ((), ())),
                preferred_element_type=F32,
            ).astype(BF16)
            at += blk


def gi_call(own, received, compress, units):
    tokens = own[0].shape[0]
    return pl.pallas_call(
        functools.partial(gi_kernel, len(own)),
        in_specs=[pl.BlockSpec(memory_space=pltpu.VMEM)] * (2 * len(own) + 1),
        out_specs=pl.BlockSpec(memory_space=pltpu.VMEM),
        out_shape=jax.ShapeDtypeStruct((tokens, units), BF16),
        compiler_params=pltpu.CompilerParams(vmem_limit_bytes=10 * MIB),
        cost_estimate=LONG,
        name="grad_input",
    )(*own, *received, compress)


def on_device(nrow, ncol, out_grad, hidden, weight, compress, feedback):
    row = lax.axis_index("row")
    col = lax.axis_index("col")
    core = col % 2
    units = weight.shape[0]
    step_tokens = out_grad.shape[0]
    after = lax.optimization_barrier

    def over_row(x, k):
        return lax.ppermute(x, "row", xor_perm(nrow, k))

    def over_col(x, k):
        return lax.ppermute(x, "col", xor_perm(ncol, k))

    idx = jnp.stack([row, core, col // 2]).astype(jnp.int32)
    grads = [out_grad] + [over_row(out_grad, k) for k in range(1, nrow)]

    def joint_perm(k):
        return [
            (r * ncol + c, (r ^ (k + c % 2)) * ncol + c) for r in range(nrow) for c in range(ncol)
        ]

    pairs = range(1, nrow - 1, 2)
    lows, lengths = [0, units // 4 * 3], [units // 4 * 3, units // 4]
    firsts, sizes = [], []
    for low, length in zip(lows, lengths):
        firsts += [lambda r, e, k=k, low=low: (r ^ (k + e)) * units + low for k in pairs]
        firsts += [
            lambda r, e, low=low, half=length // 2: (r ^ (nrow - 1)) * units + low + e * half
        ]
        sizes += [length] * len(pairs) + [length // 2]
    packed = pack_call(idx, hidden, firsts, sizes)

    def fetch(parts):
        fetched = [lax.ppermute(x, ("row", "col"), joint_perm(k)) for k, x in zip(pairs, parts)]
        return fetched + [over_row(parts[-1], nrow - 1)]

    def swap(parts):
        swapped = [over_col(x, 1) for x in parts]
        return parts[-1], swapped[-1], [x for pair in zip(parts[:-1], swapped[:-1]) for x in pair]

    early = fetch(packed[: len(pairs) + 1])
    new_feedback, *codes, ordered = compress_call(idx, grads, weight, feedback, compress, ncol)

    kept, send = [over_col(x, 1) for x in codes[2:]]
    early[-1], send = after((early[-1], send))
    *direct, packed = packed[len(pairs) + 1 :]
    packed, early[0] = after((packed, early[0]))
    early = swap(early)
    kept, send = [x.astype(F32) + y.astype(F32) for x, y in zip(codes[:2], (kept, send))]
    send, *direct = after((send.astype(BF16), *direct))
    late = fetch([*direct, packed])
    step = 1
    while True:
        received = over_col(send.astype(BF16), 2 * step)
        step *= 2
        if step == ncol // 2:
            break
        size = kept.shape[0] // 2
        send = kept[size:] + received[size:].astype(F32)
        kept = kept[:size] + received[:size].astype(F32)

    grad_weight, own, grads = gw_first(idx, hidden, *early, ordered, lows, units)
    grad_weight, kept, *late = after((grad_weight, kept, *late))
    grad_input = gi_call([kept], [received], compress, units)
    diag, swapped, pieces = swap(late)
    grad_input, swapped, *pieces = after((grad_input, swapped, *pieces))
    grad_weight = gw_last(idx, own, diag, swapped, pieces, grads, grad_weight, lows[1])
    return (grad_input, grad_weight, new_feedback)


def solution(mesh):
    return jax.shard_map(
        functools.partial(on_device, mesh.shape["row"], mesh.shape["col"]),
        mesh=mesh,
        in_specs=(P("row", "col"), P("row", None), P("row", "col"), P(), P("col", None, "row")),
        out_specs=(P("col", "row"), P("row", "col"), P("col", None, "row")),
        check_vma=False,
    )
```
